32 devices in a mesh: groups: 2 (over x), gx: 4 (over y, core), yz: 4 (over z).
Axes of the slice: x: 2, y: 2, z: 4, core: 2. Of those that a mesh axis runs over, the one named last changes fastest.
Arguments:
- hidden: bfloat16 [64, 16384], P(('groups', 'yz'), 'gx'), parts along dimension 0, may hold values from -24 to 24
- norm_gain: bfloat16 [16384], P('gx'), may hold values from 0.099609375 to 1.8984375
- w_query: bfloat16 [16384, 16384], P('gx', 'yz'), may hold values from -1 to 1
- w_key: bfloat16 [16384, 1024], P('gx', 'yz'), may hold values from -4 to 4
- w_value: bfloat16 [16384, 1024], P('gx', 'yz'), may hold values from -0.046875 to 0.046875
- w_out: bfloat16 [16384, 16384], P('yz', 'gx'), may hold values from -0.046875 to 0.046875
- key_cache: bfloat16 [64, 2048, 1024], P(('groups', 'gx'), None, 'yz'), parts along dimension 0, may hold values from -256 to 256
- value_cache: bfloat16 [64, 2048, 1024], P(('groups', 'gx'), None, 'yz'), parts along dimension 0, may hold values from -6 to 6
- cache_lengths: int32 [64], P(('groups', 'gx')), parts along dimension 0, may hold values from 128 to 2047, as said below
- positions: int32 [64], P(('groups', 'gx')), parts along dimension 0, may hold values from 2048 to 4095
Outputs:
- updated: bfloat16 [64, 16384], P(('groups', 'yz'), 'gx'), parts along dimension 0
The draws below stay inside these ranges and needn't reach their ends.
There are 2 independent parts, one for each index of `groups`. The reference program is written for one: setup_inputs(seed, part) draws one part's arguments, and reference() takes and returns one part's arrays. A program takes and returns all parts, laid end to end along the dimension named above; an argument that names none is the same for every part. Nothing has to cross between parts.
Inputs may be any that keep to these rules, and one draw needn't show every extreme that they name: Slots 0 to cache_lengths - 1 of a row are filled; some row has 2047 filled slots and some row 128.
All inputs are finite; a program needn't handle non-finite values.
Results may differ from the reference program's by a relative error of at most 0.011.
Values may be sent and summed in bfloat16 or wider, within the bound.
A program may use at most 192 MiB of HBM per device.

```python
import jax
import jax.numpy as jnp
from jax import lax

D = 16384
H = 128
KVH = 8
HD = 128
CACHE = 2048
ROWS = 32


def query_base(key):
    return jnp.clip(jax.random.normal(key, (D, KVH, H // KVH, HD), jnp.float32), -4.0, 4.0)


def draw_hidden(key, part):
    key = jax.random.fold_in(key, 11)
    base_key, row_key, col_key = jax.random.split(key, 3)
    row_scales = jnp.exp(jax.random.uniform(row_key, (ROWS, 1), jnp.float32, jnp.log(0.2), jnp.log(2.0)))
    col_scales = jnp.exp(jax.random.uniform(col_key, (1, D), jnp.float32, jnp.log(0.3), jnp.log(3.0)))
    base = jnp.clip(jax.random.normal(base_key, (ROWS, D), jnp.float32), -4.0, 4.0)
    return (base * row_scales * col_scales).astype(jnp.bfloat16)


def draw_w_query(key, part):
    shared = query_base(key)
    return (shared * D ** (-0.5)).reshape(D, H * HD).astype(jnp.bfloat16)


def draw_w_key(key, part):
    shared = query_base(key)
    key = jax.random.fold_in(key, 41)
    coupling = 2.2
    group_count = H // KVH
    noise = jnp.clip(jax.random.normal(key, (D, KVH, HD), jnp.float32), -4.0, 4.0)
    blended = coupling * jnp.sum(shared, axis=2) * group_count ** (-0.5) + noise
    return (blended * D ** (-0.5)).reshape(D, KVH * HD).astype(jnp.bfloat16)


def draw_key_cache(key, part):
    key = jax.random.fold_in(key, 23)
    base_key = jax.random.fold_in(key, 0)
    base = jnp.clip(jax.random.normal(base_key, (ROWS, CACHE, KVH, HD), jnp.float32), -4.0, 4.0)
    return base.reshape(ROWS, CACHE, KVH * HD).astype(jnp.bfloat16)


def draw_cache_lengths(key, part):
    key = jax.random.fold_in(key, 37)
    fill_key, long_key, short_key = jax.random.split(key, 3)
    lengths = jax.random.randint(fill_key, (ROWS,), CACHE // 16, CACHE, dtype=jnp.int32)
    long_row = jax.random.randint(long_key, (), 0, ROWS, dtype=jnp.int32)
    short_row = (long_row + 1 + jax.random.randint(short_key, (), 0, ROWS - 1, dtype=jnp.int32)) % ROWS
    counter = jnp.arange(ROWS, dtype=jnp.int32)
    lengths = jnp.where(counter == long_row, CACHE - 1, lengths)
    lengths = jnp.where(counter == short_row, CACHE // 16, lengths)
    return lengths.astype(jnp.int32)


def plant(array, rng, smallest, largest):
    spot = [jax.random.randint(jax.random.fold_in(rng, axis), (), 0, length) for axis, length in enumerate(array.shape)]
    widest = array.shape.index(max(array.shape))
    next_to = spot[:widest] + [(spot[widest] + 1) % array.shape[widest]] + spot[widest + 1:]
    return array.at[tuple(spot)].set(smallest).at[tuple(next_to)].set(largest)


def block_levels(key, shape, cuts, low, largest):
    gain = 1.0
    for axis_at, shards_of in cuts:
        draws = jax.random.uniform(jax.random.fold_in(jax.random.fold_in(key, 6), axis_at), (shards_of,), jnp.float32, low / len(cuts), largest / len(cuts))
        gain = gain * jnp.repeat(jnp.exp(draws), shape[axis_at] // shards_of).reshape((-1,) + (1,) * (len(shape) - 1 - axis_at))
    return gain


def centred(stream_key, shape, spread, reach, cuts=(), kind=jnp.bfloat16):
    result = jax.random.normal(stream_key, shape, jnp.float32) * spread
    if len(cuts) > 0:
        result = block_levels(stream_key, shape, cuts, -0.22, 0.18) * result
    return jnp.clip(result, min=-reach, max=reach).astype(kind)


def setup_inputs(seed: int = 0, part: int = 0) -> dict:
    key_list = jax.random.split(jax.random.key(seed), 11)
    own_keys = jax.random.split(jax.random.fold_in(key_list[10], part), 11)
    hidden = draw_hidden(jax.random.fold_in(jax.random.fold_in(key_list[10], part), 71), part)
    norm_gain = jnp.clip(1.0 + 0.18 * jax.random.normal(key_list[1], (D,), jnp.float32), 0.099609375, 1.8984375).astype(jnp.bfloat16)
    w_query = draw_w_query(jax.random.fold_in(key_list[10], 71), part)
    w_key = draw_w_key(jax.random.fold_in(key_list[10], 71), part)
    w_value = centred(key_list[4], (D, KVH * HD), D ** -0.5, 0.046875, ((0, 4), (1, 4)))
    w_out = centred(key_list[5], (H * HD, D), (H * HD) ** -0.5, 0.046875, ((0, 4), (1, 4)))
    key_cache = draw_key_cache(jax.random.fold_in(jax.random.fold_in(key_list[10], part), 71), part)
    value_cache = centred(own_keys[7], (ROWS, CACHE, KVH * HD), 1.0, 6.0, ((0, 4), (2, 4)))
    cache_lengths = draw_cache_lengths(jax.random.fold_in(jax.random.fold_in(key_list[10], part), 71), part)
    positions = plant(jax.random.randint(own_keys[9], (ROWS,), CACHE, 2 * CACHE), jax.random.fold_in(own_keys[9], 1), CACHE, (2 * CACHE) - 1).astype(jnp.int32)
    return {"hidden": hidden, "norm_gain": norm_gain, "w_query": w_query, "w_key": w_key, "w_value": w_value, "w_out": w_out, "key_cache": key_cache, "value_cache": value_cache, "cache_lengths": cache_lengths, "positions": positions}


def rotate(vectors, positions):
    half_size = vectors.shape[-1] // 2
    counter = jnp.arange(half_size, dtype=jnp.float32)
    frequency = jnp.power(jnp.float32(500000.0), -2.0 * counter / vectors.shape[-1])
    angles = positions.astype(jnp.float32)[:, None] * frequency[None, :]
    cosine = jnp.cos(angles)[:, None, :]
    sine_part = jnp.sin(angles)[:, None, :]
    lower_half = vectors[..., :half_size]
    upper_half = vectors[..., half_size:]
    return jnp.concatenate([lower_half * cosine - upper_half * sine_part, upper_half * cosine + lower_half * sine_part], axis=-1)

def attend(queries, new_key, new_value, keys, values, lengths):
    inv_root = queries.shape[-1] ** (-0.5)
    scores = jnp.einsum('rkge,rcke->rkgc', queries.astype(jnp.float32), keys.astype(jnp.float32)) * inv_root
    fresh = jnp.einsum('rkge,rke->rkg', queries.astype(jnp.float32), new_key.astype(jnp.float32)) * inv_root
    slots = jnp.arange(keys.shape[1], dtype=jnp.int32)
    valid = (slots[None, :] < lengths[:, None])[:, None, None, :]
    masked = jnp.where(valid, scores, -jnp.inf)
    highest = jnp.maximum(lax.optimization_barrier(jnp.max(masked, axis=-1)), fresh)
    weights = jnp.where(valid, jnp.exp(masked - highest[..., None]), 0.0)
    own_weight = jnp.exp(fresh - highest)
    total = lax.optimization_barrier(jnp.sum(weights, axis=-1)) + own_weight
    probs = (weights / total[..., None]).astype(jnp.bfloat16)
    own_prob = (own_weight / total).astype(jnp.bfloat16)
    mixed = jnp.einsum('rkgc,rcke->rkge', probs.astype(jnp.float32), values.astype(jnp.float32))
    mixed = mixed + own_prob.astype(jnp.float32)[..., None] * new_value.astype(jnp.float32)[:, :, None, :]
    return mixed.astype(jnp.bfloat16)

def reference(hidden, norm_gain, w_query, w_key, w_value, w_out, key_cache, value_cache, cache_lengths, positions):
    widened = hidden.astype(jnp.float32)
    row_squares = lax.optimization_barrier(jnp.sum(widened * widened, axis=1))
    inverse = lax.rsqrt(row_squares / D + 1e-05)[:, None]
    scaled = (widened * norm_gain.astype(jnp.float32)[None, :]).astype(jnp.bfloat16)
    q_part = jnp.dot(scaled, w_query, preferred_element_type=jnp.float32) * inverse
    k_part = jnp.dot(scaled, w_key, preferred_element_type=jnp.float32) * inverse
    v_part = jnp.dot(scaled, w_value, preferred_element_type=jnp.float32) * inverse
    group_size = H // KVH
    queries = rotate(q_part.reshape(ROWS, H, HD), positions).astype(jnp.bfloat16)
    queries = queries.reshape(ROWS, KVH, group_size, HD)
    new_keys = rotate(k_part.reshape(ROWS, KVH, HD), positions).astype(jnp.bfloat16)
    new_values = v_part.reshape(ROWS, KVH, HD).astype(jnp.bfloat16)
    pieces = []
    for kv_head in range(KVH):
        keys = key_cache[:, :, kv_head * HD:(kv_head + 1) * HD][:, :, None, :]
        values = value_cache[:, :, kv_head * HD:(kv_head + 1) * HD][:, :, None, :]
        mixed = attend(queries[:, kv_head:kv_head + 1], new_keys[:, kv_head:kv_head + 1], new_values[:, kv_head:kv_head + 1], keys, values, cache_lengths)
        pieces.append(mixed.reshape(ROWS, group_size * HD))
    attended = jnp.concatenate(pieces, axis=1)
    projected = jnp.dot(attended, w_out, preferred_element_type=jnp.float32)
    return (widened + projected).astype(jnp.bfloat16)
```

```python
import functools

import jax
import jax.numpy as jnp
from jax import lax
from jax.experimental import pallas as pl
from jax.experimental.pallas import tpu as pltpu
from jax.sharding import PartitionSpec as P

D = 16384
HD = 128
MESH = pl.DeviceIdType.MESH
F32 = jnp.float32
BF16 = jnp.bfloat16


def kernel(
    n_gx,
    n_yz,
    q_chunk,
    o_chunk,
    hidden,
    gain,
    w_query,
    w_key,
    w_value,
    w_out,
    key_cache,
    value_cache,
    lengths,
    cosine,
    sine,
    out,
    w_slots,
    wk_buf,
    wv_buf,
    k_buf,
    v_buf,
    x_all,
    scaled,
    sq_own,
    sq_recv,
    p_own,
    p_send,
    p_recv,
    q_rows,
    k_rows,
    v_rows,
    a_send,
    a_all,
    a_wide,
    attended,
    o_own,
    o_send,
    o_recv,
    wq_sem,
    wo_sem,
    wkv_sem,
    kc_sem,
    vc_sem,
    x_own_sem,
    x_ssem,
    x_rsem,
    sq_ssem,
    sq_rsem,
    p_ssem,
    p_rsem,
    a_ssem,
    a_rsem,
    o_ssem,
    o_rsem,
):
    gx = lax.axis_index("gx")
    yz = lax.axis_index("yz")
    q_width = w_query.shape[1]
    k_width = w_key.shape[1]
    depth = w_query.shape[0]
    o_depth, o_width = w_out.shape
    kv = k_width // HD
    heads = q_width // HD
    group = heads // kv
    nq = q_width // q_chunk
    no = o_width // o_chunk
    row_count, slot_count = key_cache.shape[0], key_cache.shape[1]
    h_rows = hidden.shape[0]
    gx_peers = [lax.rem(gx + k, n_gx) for k in range(1, n_gx)]
    yz_peers = [lax.rem(yz + k, n_yz) for k in range(1, n_yz)]

    def wq_copy(i):
        cols = pl.ds(pl.multiple_of(i * q_chunk, q_chunk), q_chunk)
        return pltpu.make_async_copy(
            w_query.at[:, cols], w_slots.at[i, pl.ds(0, depth), pl.ds(0, q_chunk)], wq_sem.at[i]
        )

    def wo_copy(i):
        cols = pl.ds(pl.multiple_of(i * o_chunk, o_chunk), o_chunk)
        return pltpu.make_async_copy(
            w_out.at[:, cols], w_slots.at[i, pl.ds(0, o_depth), pl.ds(0, o_chunk)], wo_sem.at[i]
        )

    def kc_copy(r):
        return pltpu.make_async_copy(key_cache.at[r], k_buf.at[r], kc_sem.at[r])

    def vc_copy(r):
        return pltpu.make_async_copy(value_cache.at[r], v_buf.at[r], vc_sem.at[r])

    x_own = pltpu.make_async_copy(hidden, x_all.at[yz], x_own_sem)
    x_own.start()
    barrier = pltpu.get_barrier_semaphore()
    for peer in yz_peers:
        pl.semaphore_signal(barrier, inc=1, device_id={"yz": peer}, device_id_type=MESH)
    for peer in gx_peers:
        pl.semaphore_signal(barrier, inc=1, device_id={"gx": peer}, device_id_type=MESH)
    wk_load = pltpu.make_async_copy(w_key, wk_buf, wkv_sem.at[0])
    wv_load = pltpu.make_async_copy(w_value, wv_buf, wkv_sem.at[1])
    wk_load.start()
    wv_load.start()
    for i in range(nq):
        wq_copy(i).start()
    pl.semaphore_wait(barrier, len(gx_peers) + len(yz_peers))

    def x_copy(peer, slot):
        return pltpu.make_async_remote_copy(
            src_ref=hidden,
            dst_ref=x_all.at[slot],
            send_sem=x_ssem.at[peer],
            recv_sem=x_rsem.at[slot],
            device_id={"yz": peer},
            device_id_type=MESH,
        )

    for peer in yz_peers:
        x_copy(peer, yz).start()
    x_own.wait()
    for peer in yz_peers:
        x_copy(peer, peer).wait_recv()

    step = min(depth, 512)
    squares = jnp.zeros((n_yz * h_rows, HD), F32)
    for at in range(0, depth, step):
        x = jnp.concatenate(
            [x_all[s, :, at : at + step].astype(F32) for s in range(n_yz)], axis=0
        )
        scaled[:, at : at + step] = (x * gain[:, at : at + step]).astype(BF16)
        sq = x * x
        for lane in range(0, step, HD):
            squares = squares + sq[:, lane : lane + HD]
    squares = jnp.broadcast_to(jnp.sum(squares, axis=1, keepdims=True), squares.shape)
    for d in range(n_gx):
        sq_own[d] = squares[d * row_count : (d + 1) * row_count]

    def sq_copy(peer, slot):
        return pltpu.make_async_remote_copy(
            src_ref=sq_own.at[peer],
            dst_ref=sq_recv.at[slot],
            send_sem=sq_ssem.at[peer],
            recv_sem=sq_rsem.at[slot],
            device_id={"gx": peer},
            device_id_type=MESH,
        )

    for peer in gx_peers:
        sq_copy(peer, gx).start()

    def p_copy(peer, slot, cols):
        return pltpu.make_async_remote_copy(
            src_ref=p_send.at[peer, :, cols],
            dst_ref=p_recv.at[slot, :, cols],
            send_sem=p_ssem.at[peer],
            recv_sem=p_rsem.at[slot],
            device_id={"gx": peer},
            device_id_type=MESH,
        )

    def project(weights, cols):
        y = jnp.dot(scaled[...], weights, preferred_element_type=F32)
        for d in range(n_gx):
            part = y[d * row_count : (d + 1) * row_count]
            p_own[d, :, cols] = part
            p_send[d, :, cols] = part.astype(BF16)
        for peer in gx_peers:
            p_copy(peer, gx, cols).start()

    wk_load.wait()
    project(wk_buf[...], pl.ds(q_width, k_width))
    wv_load.wait()
    project(wv_buf[...], pl.ds(q_width + k_width, k_width))

    def q_step(i, carry):
        wq_copy(i).wait()

        @pl.when(i == max(nq - 2, 0))
        def _():
            for r in range(row_count):
                kc_copy(r).start()
                vc_copy(r).start()

        cols = pl.ds(pl.multiple_of(i * q_chunk, q_chunk), q_chunk)
        project(w_slots[i, pl.ds(0, depth), pl.ds(0, q_chunk)], cols)
        return carry

    lax.fori_loop(0, nq, q_step, 0)
    early = min(2, no)
    for i in range(early):
        wo_copy(i).start()

    everything = pl.ds(0, q_width + 2 * k_width)
    sq_total = sq_own[gx]
    for peer in gx_peers:
        sq_copy(peer, peer).wait_recv()
        sq_total = sq_total + sq_recv[peer]
    inverse = lax.rsqrt(sq_total / D + 1e-05)
    for peer in gx_peers:
        p_copy(peer, peer, everything).wait_recv()
    cos, sin = cosine[...], sine[...]

    def summed(col):
        total = p_own[gx, :, col : col + HD]
        for peer in gx_peers:
            total = total + p_recv[peer, :, col : col + HD].astype(F32)
        return total * inverse

    def rope(v):
        return v * cos + pltpu.roll(v, HD // 2, 1) * sin

    for h in range(heads):
        q_rows[pl.ds(h, row_count, stride=heads), :] = rope(summed(h * HD))
    for g in range(kv):
        k_rows[pl.ds(g, row_count, stride=8), :] = rope(summed(q_width + g * HD))
        v_rows[pl.ds(g, row_count, stride=8), :] = summed(q_width + k_width + g * HD)

    def a_copy(peer, slot, r):
        return pltpu.make_async_remote_copy(
            src_ref=a_send.at[r],
            dst_ref=a_all.at[slot, r],
            send_sem=a_ssem.at[peer],
            recv_sem=a_rsem.at[slot],
            device_id={"gx": peer},
            device_id_type=MESH,
        )

    inv_root = HD ** (-0.5)

    def rounded(v):
        return v.astype(BF16).astype(F32)

    def spread(v):
        return jnp.concatenate(
            [jnp.broadcast_to(v[g : g + 1], (group, HD)) for g in range(kv)], axis=0
        )

    def row_step(r, carry):
        kc_copy(r).wait()

        if no > early:

            @pl.when(r + early < no)
            def _():
                wo_copy(jnp.minimum(r + early, no - 1)).start()

        q = rounded(q_rows[pl.ds(pl.multiple_of(r * heads, heads), heads), :])
        new_k = spread(rounded(k_rows[pl.ds(pl.multiple_of(r * 8, 8), 8), :]))
        new_v = spread(rounded(v_rows[pl.ds(pl.multiple_of(r * 8, 8), 8), :]))
        owner = lax.broadcasted_iota(jnp.int32, (heads, HD), 0) // group
        wide = jnp.concatenate(
            [jnp.where(owner == g, q, 0.0) for g in range(kv)], axis=1
        ).astype(BF16)
        scores = lax.dot_general(
            wide, k_buf[r], (((1,), (1,)), ((), ())), preferred_element_type=F32
        ) * inv_root
        fresh = jnp.sum(q * new_k, axis=1, keepdims=True) * inv_root
        slot = lax.broadcasted_iota(jnp.int32, (heads, slot_count), 1)
        masked = jnp.where(slot < lengths[r], scores, -jnp.inf)
        highest = jnp.maximum(jnp.max(masked, axis=1, keepdims=True), fresh)
        weights = jnp.exp(masked - highest)
        own = jnp.exp(fresh - highest)
        scale = 1.0 / (jnp.sum(weights, axis=1, keepdims=True) + own)
        probs = (weights * scale).astype(BF16)
        vc_copy(r).wait()
        mixed = jnp.dot(probs, v_buf[r], preferred_element_type=F32)
        mixed = jnp.concatenate(
            [
                mixed[g * group : (g + 1) * group, g * HD : (g + 1) * HD]
                for g in range(kv)
            ],
            axis=0,
        )
        mixed = (mixed + rounded(own * scale) * new_v).astype(BF16)
        a_send[r] = mixed
        a_all[gx, r] = mixed
        for peer in gx_peers:
            a_copy(peer, gx, r).start()
        return carry

    lax.fori_loop(0, row_count, row_step, 0)
    for i in range(row_count + early, no):
        wo_copy(i).start()

    def a_done(peer, slot):
        return pltpu.make_async_remote_copy(
            src_ref=a_send,
            dst_ref=a_all.at[slot],
            send_sem=a_ssem.at[peer],
            recv_sem=a_rsem.at[slot],
            device_id={"gx": peer},
            device_id_type=MESH,
        )

    for peer in gx_peers:
        a_done(peer, peer).wait_recv()
    span = row_count * heads
    for s in range(n_gx):
        for r in range(row_count):
            at = s * span + r * heads
            a_wide[at : at + heads, :] = a_all[s, r].astype(F32)
    for h in range(heads):
        attended[:, h * HD : (h + 1) * HD] = a_wide[
            pl.ds(h, n_gx * row_count, stride=heads), :
        ].astype(BF16)

    def o_copy(peer, slot, cols):
        return pltpu.make_async_remote_copy(
            src_ref=o_send.at[peer, :, cols],
            dst_ref=o_recv.at[slot, :, cols],
            send_sem=o_ssem.at[peer],
            recv_sem=o_rsem.at[slot],
            device_id={"yz": peer},
            device_id_type=MESH,
        )

    def o_step(i, carry):
        wo_copy(i).wait()
        cols = pl.ds(pl.multiple_of(i * o_chunk, o_chunk), o_chunk)
        y = jnp.dot(
            attended[...],
            w_slots[i, pl.ds(0, o_depth), pl.ds(0, o_chunk)],
            preferred_element_type=F32,
        )
        for d in range(n_yz):
            part = y[d * h_rows : (d + 1) * h_rows]
            o_own[d, :, cols] = part
            o_send[d, :, cols] = part.astype(BF16)
        for peer in yz_peers:
            o_copy(peer, yz, cols).start()
        return carry

    lax.fori_loop(0, no, o_step, 0)
    all_cols = pl.ds(0, o_width)
    for peer in yz_peers:
        o_copy(peer, peer, all_cols).wait_recv()
    for at in range(0, o_width, 512):
        total = x_all[yz, :, at : at + 512].astype(F32) + o_own[yz, :, at : at + 512]
        for peer in yz_peers:
            total = total + o_recv[peer, :, at : at + 512].astype(F32)
        out[:, at : at + 512] = total.astype(BF16)

    for peer in yz_peers:
        x_copy(peer, yz).wait_send()
        o_copy(peer, yz, all_cols).wait_send()
    for peer in gx_peers:
        sq_copy(peer, gx).wait_send()
        p_copy(peer, gx, everything).wait_send()
        a_done(peer, gx).wait_send()


def per_device(
    n_gx,
    n_yz,
    hidden,
    norm_gain,
    w_query,
    w_key,
    w_value,
    w_out,
    key_cache,
    value_cache,
    cache_lengths,
    positions,
):
    half = HD // 2
    counter = jnp.arange(half, dtype=F32)
    frequency = jnp.power(F32(500000.0), -2.0 * counter / HD)
    angles = positions.astype(F32)[:, None] * frequency[None, :]
    cosine, sine = jnp.cos(angles), jnp.sin(angles)
    cosine = jnp.concatenate([cosine, cosine], axis=1)
    sine = jnp.concatenate([-sine, sine], axis=1)
    gain = norm_gain.astype(F32)[None, :]

    h_rows = hidden.shape[0]
    depth, q_width = w_query.shape
    k_width = w_key.shape[1]
    o_depth, o_width = w_out.shape
    rows, slots, _ = key_cache.shape
    heads = q_width // HD
    q_chunk = min(512, q_width)
    o_chunk = min(512, o_width)
    nq, no = q_width // q_chunk, o_width // o_chunk
    all_rows = n_gx * rows
    p_width = q_width + 2 * k_width
    vmem = pl.BlockSpec(memory_space=pltpu.VMEM)
    smem = pl.BlockSpec(memory_space=pltpu.SMEM)
    anywhere = pl.BlockSpec(memory_space=pl.ANY)
    dma = pltpu.SemaphoreType.DMA
    return pl.pallas_call(
        functools.partial(kernel, n_gx, n_yz, q_chunk, o_chunk),
        out_shape=jax.ShapeDtypeStruct(hidden.shape, BF16),
        in_specs=[anywhere, vmem] + [anywhere] * 6 + [smem, vmem, vmem],
        out_specs=vmem,
        scratch_shapes=[
            pltpu.VMEM((max(nq, no), max(depth, o_depth), max(q_chunk, o_chunk)), BF16),
            pltpu.VMEM(w_key.shape, BF16),
            pltpu.VMEM(w_value.shape, BF16),
            pltpu.VMEM(key_cache.shape, BF16),
            pltpu.VMEM(value_cache.shape, BF16),
            pltpu.VMEM((n_yz, h_rows, depth), BF16),
            pltpu.VMEM((all_rows, depth), BF16),
            pltpu.VMEM((n_gx, rows, HD), F32),
            pltpu.VMEM((n_gx, rows, HD), F32),
            pltpu.VMEM((n_gx, rows, p_width), F32),
            pltpu.VMEM((n_gx, rows, p_width), BF16),
            pltpu.VMEM((n_gx, rows, p_width), BF16),
            pltpu.VMEM((rows * heads, HD), F32),
            pltpu.VMEM((rows * 8, HD), F32),
            pltpu.VMEM((rows * 8, HD), F32),
            pltpu.VMEM((rows, heads, HD), BF16),
            pltpu.VMEM((n_gx, rows, heads, HD), BF16),
            pltpu.VMEM((all_rows * heads, HD), F32),
            pltpu.VMEM((all_rows, o_depth), BF16),
            pltpu.VMEM((n_yz, h_rows, o_width), F32),
            pltpu.VMEM((n_yz, h_rows, o_width), BF16),
            pltpu.VMEM((n_yz, h_rows, o_width), BF16),
            dma((nq,)),
            dma((no,)),
            dma((2,)),
            dma((rows,)),
            dma((rows,)),
            dma,
            dma((n_yz,)),
            dma((n_yz,)),
            dma((n_gx,)),
            dma((n_gx,)),
            dma((n_gx,)),
            dma((n_gx,)),
            dma((n_gx,)),
            dma((n_gx,)),
            dma((n_yz,)),
            dma((n_yz,)),
        ],
        compiler_params=pltpu.CompilerParams(
            collective_id=0, has_side_effects=True, vmem_limit_bytes=62 * 2**20
        ),
    )(
        hidden,
        gain,
        w_query,
        w_key,
        w_value,
        w_out,
        key_cache,
        value_cache,
        cache_lengths,
        cosine,
        sine,
    )


def solution(mesh):
    in_specs = (
        P(("groups", "yz"), "gx"),
        P("gx"),
        P("gx", "yz"),
        P("gx", "yz"),
        P("gx", "yz"),
        P("yz", "gx"),
        P(("groups", "gx"), None, "yz"),
        P(("groups", "gx"), None, "yz"),
        P(("groups", "gx")),
        P(("groups", "gx")),
    )
    out_specs = P(("groups", "yz"), "gx")
    return jax.shard_map(
        functools.partial(per_device, mesh.shape["gx"], mesh.shape["yz"]),
        mesh=mesh,
        in_specs=in_specs,
        out_specs=out_specs,
        check_vma=False,
    )
```

```python
import functools

import jax
import jax.numpy as jnp
from jax import lax
from jax.experimental import pallas as pl
from jax.experimental.pallas import tpu as pltpu
from jax.sharding import PartitionSpec as P

D = 16384
HD = 128
MESH = pl.DeviceIdType.MESH
F32 = jnp.float32
BF16 = jnp.bfloat16


def tables(positions, rows):
    half = HD // 2
    row = lax.broadcasted_iota(jnp.int32, (rows, HD), 0)
    lane = lax.broadcasted_iota(jnp.int32, (rows, HD), 1)
    place = jnp.zeros((rows, HD), jnp.int32)
    for r in range(rows):
        place = jnp.where(row == r, positions[r], place)
    frequency = jnp.zeros((rows, HD), F32)
    for j in range(half):
        value = 500000.0 ** (-2.0 * j / HD)
        frequency = jnp.where(lane % half == j, value, frequency)
    angle = place.astype(F32) * frequency
    sine = jnp.sin(angle)
    return jnp.cos(angle), jnp.where(lane < half, -sine, sine)


def kernel(
    n_gx,
    n_yz,
    q_chunk,
    o_chunk,
    hidden,
    norm_gain,
    w_query,
    w_key,
    w_value,
    w_out,
    key_cache,
    value_cache,
    length_list,
    position_list,
    out,
    gain,
    lengths,
    positions,
    small_sem,
    w_slots,
    wk_buf,
    wv_buf,
    k_buf,
    v_buf,
    x_all,
    scaled,
    sq_own,
    sq_recv,
    p_own,
    p_send,
    p_recv,
    q_rows,
    k_rows,
    v_rows,
    a_send,
    a_all,
    a_wide,
    attended,
    o_own,
    o_send,
    o_recv,
    wq_sem,
    wo_sem,
    wkv_sem,
    kc_sem,
    vc_sem,
    x_own_sem,
    x_ssem,
    x_rsem,
    sq_ssem,
    sq_rsem,
    p_ssem,
    p_rsem,
    a_ssem,
    a_rsem,
    o_ssem,
    o_rsem,
):
    gx = lax.axis_index("gx")
    yz = lax.axis_index("yz")
    q_width = w_query.shape[1]
    k_width = w_key.shape[1]
    depth = w_query.shape[0]
    o_depth, o_width = w_out.shape
    kv = k_width // HD
    heads = q_width // HD
    group = heads // kv
    nq = q_width // q_chunk
    no = o_width // o_chunk
    row_count, slot_count = key_cache.shape[0], key_cache.shape[1]
    h_rows = hidden.shape[0]
    gx_peers = [lax.rem(gx + k, n_gx) for k in range(1, n_gx)]
    yz_peers = [lax.rem(yz + k, n_yz) for k in range(1, n_yz)]

    def wq_copy(i):
        cols = pl.ds(pl.multiple_of(i * q_chunk, q_chunk), q_chunk)
        return pltpu.make_async_copy(
            w_query.at[:, cols], w_slots.at[i, pl.ds(0, depth), pl.ds(0, q_chunk)], wq_sem.at[i]
        )

    def wo_copy(i):
        cols = pl.ds(pl.multiple_of(i * o_chunk, o_chunk), o_chunk)
        return pltpu.make_async_copy(
            w_out.at[:, cols], w_slots.at[i, pl.ds(0, o_depth), pl.ds(0, o_chunk)], wo_sem.at[i]
        )

    def kc_copy(r):
        return pltpu.make_async_copy(key_cache.at[r], k_buf.at[r], kc_sem.at[r])

    def vc_copy(r):
        return pltpu.make_async_copy(value_cache.at[r], v_buf.at[r], vc_sem.at[r])

    x_own = pltpu.make_async_copy(hidden, x_all.at[yz], x_own_sem)
    x_own.start()
    barrier = pltpu.get_barrier_semaphore()
    for peer in yz_peers:
        pl.semaphore_signal(barrier, inc=1, device_id={"yz": peer}, device_id_type=MESH)
    for peer in gx_peers:
        pl.semaphore_signal(barrier, inc=1, device_id={"gx": peer}, device_id_type=MESH)
    small = [
        pltpu.make_async_copy(a, b, small_sem.at[i])
        for i, (a, b) in enumerate(
            [(norm_gain, gain), (length_list, lengths), (position_list, positions)]
        )
    ]
    for load in small:
        load.start()
    wk_load = pltpu.make_async_copy(w_key, wk_buf, wkv_sem.at[0])
    wv_load = pltpu.make_async_copy(w_value, wv_buf, wkv_sem.at[1])
    wk_load.start()
    wv_load.start()
    for i in range(nq):
        wq_copy(i).start(priority=1)
    for r in range(row_count):
        kc_copy(r).start(priority=1)
        vc_copy(r).start(priority=1)
    pl.semaphore_wait(barrier, len(gx_peers) + len(yz_peers))

    def x_copy(peer, slot):
        return pltpu.make_async_remote_copy(
            src_ref=x_all.at[yz],
            dst_ref=x_all.at[slot],
            send_sem=x_ssem.at[peer],
            recv_sem=x_rsem.at[slot],
            device_id={"yz": peer},
            device_id_type=MESH,
        )

    x_own.wait()
    for peer in yz_peers:
        x_copy(peer, yz).start()
    for load in small:
        load.wait()
    cos, sin = tables(positions, row_count)
    for peer in yz_peers:
        x_copy(peer, peer).wait_recv()

    step = min(depth, 512)
    gains = gain[...].astype(F32)
    squares = jnp.zeros((n_yz * h_rows, HD), F32)
    for at in range(0, depth, step):
        x = jnp.concatenate(
            [x_all[s, :, at : at + step].astype(F32) for s in range(n_yz)], axis=0
        )
        sq = x * x
        for lane in range(0, step, HD):
            squares = squares + sq[:, lane : lane + HD]
            j = (at + lane) // HD
            part = x[:, lane : lane + HD] * gains[j : j + 1]
            scaled[:, at + lane : at + lane + HD] = part.astype(BF16)
    squares = jnp.broadcast_to(jnp.sum(squares, axis=1, keepdims=True), squares.shape)
    for d in range(n_gx):
        sq_own[d] = squares[d * row_count : (d + 1) * row_count]

    def sq_copy(peer, slot):
        return pltpu.make_async_remote_copy(
            src_ref=sq_own.at[peer],
            dst_ref=sq_recv.at[slot],
            send_sem=sq_ssem.at[peer],
            recv_sem=sq_rsem.at[slot],
            device_id={"gx": peer},
            device_id_type=MESH,
        )

    for peer in gx_peers:
        sq_copy(peer, gx).start()

    def p_copy(peer, slot, cols):
        return pltpu.make_async_remote_copy(
            src_ref=p_send.at[peer, :, cols],
            dst_ref=p_recv.at[slot, :, cols],
            send_sem=p_ssem.at[peer],
            recv_sem=p_rsem.at[slot],
            device_id={"gx": peer},
            device_id_type=MESH,
        )

    def project(weights, cols):
        y = jnp.dot(scaled[...], weights, preferred_element_type=F32)
        for d in range(n_gx):
            part = y[d * row_count : (d + 1) * row_count]
            p_own[d, :, cols] = part
            p_send[d, :, cols] = part.astype(BF16)
        for peer in gx_peers:
            p_copy(peer, gx, cols).start()

    wk_load.wait()
    project(wk_buf[...], pl.ds(q_width, k_width))
    wv_load.wait()
    project(wv_buf[...], pl.ds(q_width + k_width, k_width))

    def q_step(i, carry):
        wq_copy(i).wait()

        cols = pl.ds(pl.multiple_of(i * q_chunk, q_chunk), q_chunk)
        project(w_slots[i, pl.ds(0, depth), pl.ds(0, q_chunk)], cols)

        @pl.when(i < no)
        def _():
            wo_copy(jnp.minimum(i, no - 1)).start(priority=1)

        return carry

    lax.fori_loop(0, nq, q_step, 0)
    for i in range(nq, no):
        wo_copy(i).start(priority=1)

    everything = pl.ds(0, q_width + 2 * k_width)
    sq_total = sq_own[gx]
    for peer in gx_peers:
        sq_copy(peer, peer).wait_recv()
        sq_total = sq_total + sq_recv[peer]
    inverse = lax.rsqrt(sq_total / D + 1e-05)
    for peer in gx_peers:
        p_copy(peer, peer, everything).wait_recv()

    def summed(col):
        total = p_own[gx, :, col : col + HD]
        for peer in gx_peers:
            total = total + p_recv[peer, :, col : col + HD].astype(F32)
        return total * inverse

    def rope(v):
        return v * cos + pltpu.roll(v, HD // 2, 1) * sin

    for h in range(heads):
        q_rows[pl.ds(h, row_count, stride=heads), :] = rope(summed(h * HD))
    for g in range(kv):
        k_rows[pl.ds(g, row_count, stride=8), :] = rope(summed(q_width + g * HD))
        v_rows[pl.ds(g, row_count, stride=8), :] = summed(q_width + k_width + g * HD)

    def a_copy(peer, slot, r):
        return pltpu.make_async_remote_copy(
            src_ref=a_send.at[r],
            dst_ref=a_all.at[slot, r],
            send_sem=a_ssem.at[peer],
            recv_sem=a_rsem.at[slot],
            device_id={"gx": peer},
            device_id_type=MESH,
        )

    inv_root = HD ** (-0.5)

    def rounded(v):
        return v.astype(BF16).astype(F32)

    def spread(v):
        return jnp.concatenate(
            [jnp.broadcast_to(v[g : g + 1], (group, HD)) for g in range(kv)], axis=0
        )

    def row_step(r, carry):
        kc_copy(r).wait()

        q = rounded(q_rows[pl.ds(pl.multiple_of(r * heads, heads), heads), :])
        new_k = spread(rounded(k_rows[pl.ds(pl.multiple_of(r * 8, 8), 8), :]))
        new_v = spread(rounded(v_rows[pl.ds(pl.multiple_of(r * 8, 8), 8), :]))
        owner = lax.broadcasted_iota(jnp.int32, (heads, HD), 0) // group
        wide = jnp.concatenate(
            [jnp.where(owner == g, q, 0.0) for g in range(kv)], axis=1
        ).astype(BF16)
        scores = lax.dot_general(
            wide, k_buf[r], (((1,), (1,)), ((), ())), preferred_element_type=F32
        ) * inv_root
        fresh = jnp.sum(q * new_k, axis=1, keepdims=True) * inv_root
        slot = lax.broadcasted_iota(jnp.int32, (heads, slot_count), 1)
        masked = jnp.where(slot < lengths[r], scores, -jnp.inf)
        highest = jnp.maximum(jnp.max(masked, axis=1, keepdims=True), fresh)
        weights = jnp.exp(masked - highest)
        own = jnp.exp(fresh - highest)
        scale = 1.0 / (jnp.sum(weights, axis=1, keepdims=True) + own)
        probs = (weights * scale).astype(BF16)
        vc_copy(r).wait()
        mixed = jnp.dot(probs, v_buf[r], preferred_element_type=F32)
        mixed = jnp.concatenate(
            [
                mixed[g * group : (g + 1) * group, g * HD : (g + 1) * HD]
                for g in range(kv)
            ],
            axis=0,
        )
        mixed = (mixed + rounded(own * scale) * new_v).astype(BF16)
        a_send[r] = mixed
        a_all[gx, r] = mixed
        for peer in gx_peers:
            a_copy(peer, gx, r).start()
        return carry

    lax.fori_loop(0, row_count, row_step, 0, unroll=True)
    def a_done(peer, slot):
        return pltpu.make_async_remote_copy(
            src_ref=a_send,
            dst_ref=a_all.at[slot],
            send_sem=a_ssem.at[peer],
            recv_sem=a_rsem.at[slot],
            device_id={"gx": peer},
            device_id_type=MESH,
        )

    for peer in gx_peers:
        a_done(peer, peer).wait_recv()
    span = row_count * heads
    for s in range(n_gx):
        for r in range(row_count):
            at = s * span + r * heads
            a_wide[at : at + heads, :] = a_all[s, r].astype(F32)
    for h in range(heads):
        attended[:, h * HD : (h + 1) * HD] = a_wide[
            pl.ds(h, n_gx * row_count, stride=heads), :
        ].astype(BF16)

    def o_copy(peer, slot, cols):
        return pltpu.make_async_remote_copy(
            src_ref=o_send.at[peer, :, cols],
            dst_ref=o_recv.at[slot, :, cols],
            send_sem=o_ssem.at[peer],
            recv_sem=o_rsem.at[slot],
            device_id={"yz": peer},
            device_id_type=MESH,
        )

    def o_step(i, carry):
        wo_copy(i).wait()
        cols = pl.ds(pl.multiple_of(i * o_chunk, o_chunk), o_chunk)
        y = jnp.dot(
            attended[...],
            w_slots[i, pl.ds(0, o_depth), pl.ds(0, o_chunk)],
            preferred_element_type=F32,
        )
        for d in range(n_yz):
            part = y[d * h_rows : (d + 1) * h_rows]
            o_own[d, :, cols] = part
            o_send[d, :, cols] = part.astype(BF16)
        for peer in yz_peers:
            o_copy(peer, yz, cols).start()
        return carry

    lax.fori_loop(0, no, o_step, 0)
    all_cols = pl.ds(0, o_width)
    for peer in yz_peers:
        o_copy(peer, peer, all_cols).wait_recv()
    for at in range(0, o_width, 512):
        total = x_all[yz, :, at : at + 512].astype(F32) + o_own[yz, :, at : at + 512]
        for peer in yz_peers:
            total = total + o_recv[peer, :, at : at + 512].astype(F32)
        out[:, at : at + 512] = total.astype(BF16)

    for peer in yz_peers:
        x_copy(peer, yz).wait_send()
        o_copy(peer, yz, all_cols).wait_send()
    for peer in gx_peers:
        sq_copy(peer, gx).wait_send()
        p_copy(peer, gx, everything).wait_send()
        a_done(peer, gx).wait_send()


def per_device(
    n_gx,
    n_yz,
    hidden,
    norm_gain,
    w_query,
    w_key,
    w_value,
    w_out,
    key_cache,
    value_cache,
    cache_lengths,
    positions,
):
    gain = norm_gain.reshape(-1, HD)
    h_rows = hidden.shape[0]
    depth, q_width = w_query.shape
    k_width = w_key.shape[1]
    o_depth, o_width = w_out.shape
    rows, slots, _ = key_cache.shape
    heads = q_width // HD
    q_chunk = min(512, q_width)
    o_chunk = min(512, o_width)
    nq, no = q_width // q_chunk, o_width // o_chunk
    all_rows = n_gx * rows
    p_width = q_width + 2 * k_width
    vmem = pl.BlockSpec(memory_space=pltpu.VMEM)
    anywhere = pl.BlockSpec(memory_space=pl.ANY)
    dma = pltpu.SemaphoreType.DMA
    return pl.pallas_call(
        functools.partial(kernel, n_gx, n_yz, q_chunk, o_chunk),
        out_shape=jax.ShapeDtypeStruct(hidden.shape, BF16),
        in_specs=[anywhere] * 10,
        out_specs=vmem,
        scratch_shapes=[
            pltpu.VMEM(gain.shape, BF16),
            pltpu.SMEM(cache_lengths.shape, jnp.int32),
            pltpu.SMEM(positions.shape, jnp.int32),
            dma((3,)),
            pltpu.VMEM((max(nq, no), max(depth, o_depth), max(q_chunk, o_chunk)), BF16),
            pltpu.VMEM(w_key.shape, BF16),
            pltpu.VMEM(w_value.shape, BF16),
            pltpu.VMEM(key_cache.shape, BF16),
            pltpu.VMEM(value_cache.shape, BF16),
            pltpu.VMEM((n_yz, h_rows, depth), BF16),
            pltpu.VMEM((all_rows, depth), BF16),
            pltpu.VMEM((n_gx, rows, HD), F32),
            pltpu.VMEM((n_gx, rows, HD), F32),
            pltpu.VMEM((n_gx, rows, p_width), F32),
            pltpu.VMEM((n_gx, rows, p_width), BF16),
            pltpu.VMEM((n_gx, rows, p_width), BF16),
            pltpu.VMEM((rows * heads, HD), F32),
            pltpu.VMEM((rows * 8, HD), F32),
            pltpu.VMEM((rows * 8, HD), F32),
            pltpu.VMEM((rows, heads, HD), BF16),
            pltpu.VMEM((n_gx, rows, heads, HD), BF16),
            pltpu.VMEM((all_rows * heads, HD), F32),
            pltpu.VMEM((all_rows, o_depth), BF16),
            pltpu.VMEM((n_yz, h_rows, o_width), F32),
            pltpu.VMEM((n_yz, h_rows, o_width), BF16),
            pltpu.VMEM((n_yz, h_rows, o_width), BF16),
            dma((nq,)),
            dma((no,)),
            dma((2,)),
            dma((rows,)),
            dma((rows,)),
            dma,
            dma((n_yz,)),
            dma((n_yz,)),
            dma((n_gx,)),
            dma((n_gx,)),
            dma((n_gx,)),
            dma((n_gx,)),
            dma((n_gx,)),
            dma((n_gx,)),
            dma((n_yz,)),
            dma((n_yz,)),
        ],
        compiler_params=pltpu.CompilerParams(
            collective_id=0, has_side_effects=True, vmem_limit_bytes=62 * 2**20
        ),
    )(
        hidden,
        gain,
        w_query,
        w_key,
        w_value,
        w_out,
        key_cache,
        value_cache,
        cache_lengths,
        positions,
    )


def solution(mesh):
    in_specs = (
        P(("groups", "yz"), "gx"),
        P("gx"),
        P("gx", "yz"),
        P("gx", "yz"),
        P("gx", "yz"),
        P("yz", "gx"),
        P(("groups", "gx"), None, "yz"),
        P(("groups", "gx"), None, "yz"),
        P(("groups", "gx")),
        P(("groups", "gx")),
    )
    out_specs = P(("groups", "yz"), "gx")
    return jax.shard_map(
        functools.partial(per_device, mesh.shape["gx"], mesh.shape["yz"]),
        mesh=mesh,
        in_specs=in_specs,
        out_specs=out_specs,
        check_vma=False,
    )
```

```python
import functools

import jax
import jax.numpy as jnp
from jax import lax
from jax.experimental import pallas as pl
from jax.experimental.pallas import tpu as pltpu
from jax.sharding import PartitionSpec as P

D = 16384
HD = 128
MESH = pl.DeviceIdType.MESH
F32 = jnp.float32
BF16 = jnp.bfloat16


def tables(positions, rows):
    half = HD // 2
    row = lax.broadcasted_iota(jnp.int32, (rows, HD), 0)
    lane = lax.broadcasted_iota(jnp.int32, (rows, HD), 1)
    place = jnp.zeros((rows, HD), jnp.int32)
    for r in range(rows):
        place = jnp.where(row == r, positions[r], place)
    frequency = jnp.zeros((rows, HD), F32)
    for j in range(half):
        value = 500000.0 ** (-2.0 * j / HD)
        frequency = jnp.where(lane % half == j, value, frequency)
    angle = place.astype(F32) * frequency
    sine = jnp.sin(angle)
    return jnp.cos(angle), jnp.where(lane < half, -sine, sine)


def kernel(
    n_gx,
    n_yz,
    q_chunk,
    o_chunk,
    hidden,
    norm_gain,
    w_query,
    w_key,
    w_value,
    w_out,
    key_cache,
    value_cache,
    length_list,
    position_list,
    out,
    gain,
    lengths,
    positions,
    small_sem,
    w_slots,
    wk_buf,
    wv_buf,
    k_buf,
    v_buf,
    x_all,
    scaled,
    sq_own,
    sq_recv,
    p_own,
    p_send,
    p_recv,
    q_rows,
    k_rows,
    v_rows,
    a_send,
    a_all,
    a_wide,
    attended,
    o_own,
    o_send,
    o_recv,
    wq_sem,
    wo_sem,
    wkv_sem,
    kc_sem,
    vc_sem,
    x_own_sem,
    x_ssem,
    x_rsem,
    sq_ssem,
    sq_rsem,
    p_ssem,
    p_rsem,
    a_ssem,
    a_rsem,
    o_ssem,
    o_rsem,
):
    gx = lax.axis_index("gx")
    yz = lax.axis_index("yz")
    q_width = w_query.shape[1]
    k_width = w_key.shape[1]
    depth = w_query.shape[0]
    o_depth, o_width = w_out.shape
    kv = k_width // HD
    heads = q_width // HD
    group = heads // kv
    nq = q_width // q_chunk
    no = o_width // o_chunk
    row_count, slot_count = key_cache.shape[0], key_cache.shape[1]
    h_rows = hidden.shape[0]
    gx_peers = [lax.rem(gx + k, n_gx) for k in range(1, n_gx)]
    yz_peers = [lax.rem(yz + k, n_yz) for k in range(1, n_yz)]

    def wq_copy(i):
        cols = pl.ds(pl.multiple_of(i * q_chunk, q_chunk), q_chunk)
        return pltpu.make_async_copy(
            w_query.at[:, cols], w_slots.at[i, pl.ds(0, depth), pl.ds(0, q_chunk)], wq_sem.at[i]
        )

    def wo_copy(i):
        cols = pl.ds(pl.multiple_of(i * o_chunk, o_chunk), o_chunk)
        return pltpu.make_async_copy(
            w_out.at[:, cols], w_slots.at[i, pl.ds(0, o_depth), pl.ds(0, o_chunk)], wo_sem.at[i]
        )

    def kc_copy(r):
        return pltpu.make_async_copy(key_cache.at[r], k_buf.at[r], kc_sem.at[r])

    def vc_copy(r):
        return pltpu.make_async_copy(value_cache.at[r], v_buf.at[r], vc_sem.at[r])

    x_own = pltpu.make_async_copy(hidden, x_all.at[yz], x_own_sem)
    x_own.start()
    barrier = pltpu.get_barrier_semaphore()
    for peer in yz_peers:
        pl.semaphore_signal(barrier, inc=1, device_id={"yz": peer}, device_id_type=MESH)
    for peer in gx_peers:
        pl.semaphore_signal(barrier, inc=1, device_id={"gx": peer}, device_id_type=MESH)
    small = [
        pltpu.make_async_copy(a, b, small_sem.at[i])
        for i, (a, b) in enumerate(
            [(norm_gain, gain), (length_list, lengths), (position_list, positions)]
        )
    ]
    for load in small:
        load.start()
    wk_load = pltpu.make_async_copy(w_key, wk_buf, wkv_sem.at[0])
    wv_load = pltpu.make_async_copy(w_value, wv_buf, wkv_sem.at[1])
    wk_load.start()
    wv_load.start()
    for i in range(nq):
        wq_copy(i).start(priority=1)
    for r in range(row_count):
        kc_copy(r).start(priority=1)
        vc_copy(r).start(priority=1)
    pl.semaphore_wait(barrier, len(gx_peers) + len(yz_peers))

    def x_copy(peer, slot):
        return pltpu.make_async_remote_copy(
            src_ref=x_all.at[yz],
            dst_ref=x_all.at[slot],
            send_sem=x_ssem.at[peer],
            recv_sem=x_rsem.at[slot],
            device_id={"yz": peer},
            device_id_type=MESH,
        )

    x_own.wait()
    for peer in yz_peers:
        x_copy(peer, yz).start()
    for load in small:
        load.wait()
    cos, sin = tables(positions, row_count)
    for peer in yz_peers:
        x_copy(peer, peer).wait_recv()

    step = min(depth, 512)
    gains = gain[...].astype(F32)
    squares = jnp.zeros((n_yz * h_rows, HD), F32)
    for at in range(0, depth, step):
        x = jnp.concatenate(
            [x_all[s, :, at : at + step].astype(F32) for s in range(n_yz)], axis=0
        )
        sq = x * x
        for lane in range(0, step, HD):
            squares = squares + sq[:, lane : lane + HD]
            j = (at + lane) // HD
            part = x[:, lane : lane + HD] * gains[j : j + 1]
            scaled[:, at + lane : at + lane + HD] = part.astype(BF16)
    squares = jnp.broadcast_to(jnp.sum(squares, axis=1, keepdims=True), squares.shape)
    for d in range(n_gx):
        sq_own[d] = squares[d * row_count : (d + 1) * row_count]

    def sq_copy(peer, slot):
        return pltpu.make_async_remote_copy(
            src_ref=sq_own.at[peer],
            dst_ref=sq_recv.at[slot],
            send_sem=sq_ssem.at[peer],
            recv_sem=sq_rsem.at[slot],
            device_id={"gx": peer},
            device_id_type=MESH,
        )

    for peer in gx_peers:
        sq_copy(peer, gx).start()

    def p_copy(peer, slot, cols):
        return pltpu.make_async_remote_copy(
            src_ref=p_send.at[peer, :, cols],
            dst_ref=p_recv.at[slot, :, cols],
            send_sem=p_ssem.at[peer],
            recv_sem=p_rsem.at[slot],
            device_id={"gx": peer},
            device_id_type=MESH,
        )

    def project(weights, cols):
        y = jnp.dot(scaled[...], weights, preferred_element_type=F32)
        for d in range(n_gx):
            part = y[d * row_count : (d + 1) * row_count]
            p_own[d, :, cols] = part
            p_send[d, :, cols] = part.astype(BF16)
        for peer in gx_peers:
            p_copy(peer, gx, cols).start()

    wk_load.wait()
    project(wk_buf[...], pl.ds(q_width, k_width))
    wv_load.wait()
    project(wv_buf[...], pl.ds(q_width + k_width, k_width))

    def q_step(i, carry):
        wq_copy(i).wait()

        cols = pl.ds(pl.multiple_of(i * q_chunk, q_chunk), q_chunk)
        project(w_slots[i, pl.ds(0, depth), pl.ds(0, q_chunk)], cols)

        @pl.when(i < no)
        def _():
            wo_copy(jnp.minimum(i, no - 1)).start(priority=1)

        return carry

    lax.fori_loop(0, nq, q_step, 0)
    for i in range(nq, no):
        wo_copy(i).start(priority=1)

    everything = pl.ds(0, q_width + 2 * k_width)
    sq_total = sq_own[gx]
    for peer in gx_peers:
        sq_copy(peer, peer).wait_recv()
        sq_total = sq_total + sq_recv[peer]
    inverse = lax.rsqrt(sq_total / D + 1e-05)
    for peer in gx_peers:
        p_copy(peer, peer, everything).wait_recv()

    def summed(col):
        total = p_own[gx, :, col : col + HD]
        for peer in gx_peers:
            total = total + p_recv[peer, :, col : col + HD].astype(F32)
        return total * inverse

    def rope(v):
        return v * cos + pltpu.roll(v, HD // 2, 1) * sin

    for h in range(heads):
        q_rows[pl.ds(h, row_count, stride=heads), :] = rope(summed(h * HD))
    for g in range(kv):
        k_rows[pl.ds(g, row_count, stride=8), :] = rope(summed(q_width + g * HD))
        v_rows[pl.ds(g, row_count, stride=8), :] = summed(q_width + k_width + g * HD)

    def a_copy(peer, slot, r):
        return pltpu.make_async_remote_copy(
            src_ref=a_send.at[r],
            dst_ref=a_all.at[slot, r],
            send_sem=a_ssem.at[peer],
            recv_sem=a_rsem.at[slot],
            device_id={"gx": peer},
            device_id_type=MESH,
        )

    inv_root = HD ** (-0.5)

    def rounded(v):
        return v.astype(BF16).astype(F32)

    def spread(v):
        return jnp.concatenate(
            [jnp.broadcast_to(v[g : g + 1], (group, HD)) for g in range(kv)], axis=0
        )

    def row_step(r, carry):
        kc_copy(r).wait()

        q = rounded(q_rows[pl.ds(pl.multiple_of(r * heads, heads), heads), :])
        new_k = spread(rounded(k_rows[pl.ds(pl.multiple_of(r * 8, 8), 8), :]))
        new_v = spread(rounded(v_rows[pl.ds(pl.multiple_of(r * 8, 8), 8), :]))
        owner = lax.broadcasted_iota(jnp.int32, (heads, HD), 0) // group
        wide = jnp.concatenate(
            [jnp.where(owner == g, q, 0.0) for g in range(kv)], axis=1
        ).astype(BF16)
        scores = lax.dot_general(
            wide, k_buf[r], (((1,), (1,)), ((), ())), preferred_element_type=F32
        ) * inv_root
        fresh = jnp.sum(q * new_k, axis=1, keepdims=True) * inv_root
        slot = lax.broadcasted_iota(jnp.int32, (heads, slot_count), 1)
        masked = jnp.where(slot < lengths[r], scores, -jnp.inf)
        highest = jnp.maximum(jnp.max(masked, axis=1, keepdims=True), fresh)
        weights = jnp.exp(masked - highest)
        own = jnp.exp(fresh - highest)
        scale = 1.0 / (jnp.sum(weights, axis=1, keepdims=True) + own)
        probs = (weights * scale).astype(BF16)
        vc_copy(r).wait()
        mixed = jnp.dot(probs, v_buf[r], preferred_element_type=F32)
        mixed = jnp.concatenate(
            [
                mixed[g * group : (g + 1) * group, g * HD : (g + 1) * HD]
                for g in range(kv)
            ],
            axis=0,
        )
        mixed = (mixed + rounded(own * scale) * new_v).astype(BF16)
        a_send[r] = mixed
        a_all[gx, r] = mixed
        for peer in gx_peers:
            a_copy(peer, gx, r).start()
        return carry

    lax.fori_loop(0, row_count, row_step, 0, unroll=True)
    def a_done(peer, slot):
        return pltpu.make_async_remote_copy(
            src_ref=a_send,
            dst_ref=a_all.at[slot],
            send_sem=a_ssem.at[peer],
            recv_sem=a_rsem.at[slot],
            device_id={"gx": peer},
            device_id_type=MESH,
        )

    for peer in gx_peers:
        a_done(peer, peer).wait_recv()
    span = row_count * heads
    for s in range(n_gx):
        for r in range(row_count):
            at = s * span + r * heads
            a_wide[at : at + heads, :] = a_all[s, r].astype(F32)
    for h in range(heads):
        attended[:, h * HD : (h + 1) * HD] = a_wide[
            pl.ds(h, n_gx * row_count, stride=heads), :
        ].astype(BF16)

    def o_copy(peer, slot, cols):
        return pltpu.make_async_remote_copy(
            src_ref=o_send.at[peer, :, cols],
            dst_ref=o_recv.at[slot, :, cols],
            send_sem=o_ssem.at[peer],
            recv_sem=o_rsem.at[slot],
            device_id={"yz": peer},
            device_id_type=MESH,
        )

    def o_step(i, carry):
        wo_copy(i).wait()
        cols = pl.ds(pl.multiple_of(i * o_chunk, o_chunk), o_chunk)
        y = jnp.dot(
            attended[...],
            w_slots[i, pl.ds(0, o_depth), pl.ds(0, o_chunk)],
            preferred_element_type=F32,
        )
        for d in range(n_yz):
            part = y[d * h_rows : (d + 1) * h_rows]
            o_own[d, :, cols] = part
            o_send[d, :, cols] = part.astype(BF16)
        for peer in yz_peers:
            o_copy(peer, yz, cols).start()
        return carry

    lax.fori_loop(0, no, o_step, 0, unroll=2)
    all_cols = pl.ds(0, o_width)
    for peer in yz_peers:
        o_copy(peer, peer, all_cols).wait_recv()
    for at in range(0, o_width, 512):
        total = x_all[yz, :, at : at + 512].astype(F32) + o_own[yz, :, at : at + 512]
        for peer in yz_peers:
            total = total + o_recv[peer, :, at : at + 512].astype(F32)
        out[:, at : at + 512] = total.astype(BF16)

    for peer in yz_peers:
        x_copy(peer, yz).wait_send()
        o_copy(peer, yz, all_cols).wait_send()
    for peer in gx_peers:
        sq_copy(peer, gx).wait_send()
        p_copy(peer, gx, everything).wait_send()
        a_done(peer, gx).wait_send()


def per_device(
    n_gx,
    n_yz,
    hidden,
    norm_gain,
    w_query,
    w_key,
    w_value,
    w_out,
    key_cache,
    value_cache,
    cache_lengths,
    positions,
):
    gain = norm_gain.reshape(-1, HD)
    h_rows = hidden.shape[0]
    depth, q_width = w_query.shape
    k_width = w_key.shape[1]
    o_depth, o_width = w_out.shape
    rows, slots, _ = key_cache.shape
    heads = q_width // HD
    q_chunk = min(512, q_width)
    o_chunk = min(512, o_width)
    nq, no = q_width // q_chunk, o_width // o_chunk
    all_rows = n_gx * rows
    p_width = q_width + 2 * k_width
    vmem = pl.BlockSpec(memory_space=pltpu.VMEM)
    anywhere = pl.BlockSpec(memory_space=pl.ANY)
    dma = pltpu.SemaphoreType.DMA
    return pl.pallas_call(
        functools.partial(kernel, n_gx, n_yz, q_chunk, o_chunk),
        out_shape=jax.ShapeDtypeStruct(hidden.shape, BF16),
        in_specs=[anywhere] * 10,
        out_specs=vmem,
        scratch_shapes=[
            pltpu.VMEM(gain.shape, BF16),
            pltpu.SMEM(cache_lengths.shape, jnp.int32),
            pltpu.SMEM(positions.shape, jnp.int32),
            dma((3,)),
            pltpu.VMEM((max(nq, no), max(depth, o_depth), max(q_chunk, o_chunk)), BF16),
            pltpu.VMEM(w_key.shape, BF16),
            pltpu.VMEM(w_value.shape, BF16),
            pltpu.VMEM(key_cache.shape, BF16),
            pltpu.VMEM(value_cache.shape, BF16),
            pltpu.VMEM((n_yz, h_rows, depth), BF16),
            pltpu.VMEM((all_rows, depth), BF16),
            pltpu.VMEM((n_gx, rows, HD), F32),
            pltpu.VMEM((n_gx, rows, HD), F32),
            pltpu.VMEM((n_gx, rows, p_width), F32),
            pltpu.VMEM((n_gx, rows, p_width), BF16),
            pltpu.VMEM((n_gx, rows, p_width), BF16),
            pltpu.VMEM((rows * heads, HD), F32),
            pltpu.VMEM((rows * 8, HD), F32),
            pltpu.VMEM((rows * 8, HD), F32),
            pltpu.VMEM((rows, heads, HD), BF16),
            pltpu.VMEM((n_gx, rows, heads, HD), BF16),
            pltpu.VMEM((all_rows * heads, HD), F32),
            pltpu.VMEM((all_rows, o_depth), BF16),
            pltpu.VMEM((n_yz, h_rows, o_width), F32),
            pltpu.VMEM((n_yz, h_rows, o_width), BF16),
            pltpu.VMEM((n_yz, h_rows, o_width), BF16),
            dma((nq,)),
            dma((no,)),
            dma((2,)),
            dma((rows,)),
            dma((rows,)),
            dma,
            dma((n_yz,)),
            dma((n_yz,)),
            dma((n_gx,)),
            dma((n_gx,)),
            dma((n_gx,)),
            dma((n_gx,)),
            dma((n_gx,)),
            dma((n_gx,)),
            dma((n_yz,)),
            dma((n_yz,)),
        ],
        compiler_params=pltpu.CompilerParams(
            collective_id=0, has_side_effects=True, vmem_limit_bytes=62 * 2**20
        ),
    )(
        hidden,
        gain,
        w_query,
        w_key,
        w_value,
        w_out,
        key_cache,
        value_cache,
        cache_lengths,
        positions,
    )


def solution(mesh):
    in_specs = (
        P(("groups", "yz"), "gx"),
        P("gx"),
        P("gx", "yz"),
        P("gx", "yz"),
        P("gx", "yz"),
        P("yz", "gx"),
        P(("groups", "gx"), None, "yz"),
        P(("groups", "gx"), None, "yz"),
        P(("groups", "gx")),
        P(("groups", "gx")),
    )
    out_specs = P(("groups", "yz"), "gx")
    return jax.shard_map(
        functools.partial(per_device, mesh.shape["gx"], mesh.shape["yz"]),
        mesh=mesh,
        in_specs=in_specs,
        out_specs=out_specs,
        check_vma=False,
    )
```
